32 devices in a mesh: groups: 2 (over y), section: 4 (over z), fsdp: 4 (over x, core).
Axes of the slice: x: 2, y: 2, z: 4, core: 2. Of those that a mesh axis runs over, the one named last changes fastest.
Arguments:
- sent_act: bfloat16 [4, 1024, 4096], P('section', 'groups', 'fsdp'), parts along dimension 1, may hold values from -6 to 6
- sent_grad: bfloat16 [4, 1024, 4096], P('section', 'groups', 'fsdp'), parts along dimension 1, may hold values from -6 to 6
- stash_in: bfloat16 [4, 2, 1024, 4096], P('section', None, 'groups', 'fsdp'), parts along dimension 2, may hold values from -6 to 6
- stash_pre: bfloat16 [4, 2, 1024, 4096], P('section', None, 'groups', 'fsdp'), parts along dimension 2, may hold values from -6 to 6
- layer_weight: bfloat16 [4, 4096, 4096], P('section', None, 'fsdp'), may hold values from -0.125 to 0.125
- layer_bias: float32 [4, 4096], P('section', 'fsdp'), may hold values from -3 to 3
- seg_table: bfloat16 [4784, 4096], P('section', 'fsdp'), may hold values from -6 to 6
- seg_index: int32 [1024, 32], P('groups'), parts along dimension 0, may hold values from 0 to 4783
- seg_amp: float32 [1024, 32], P('groups'), parts along dimension 0, may hold values from -1.2 to 1.2
- field_angle: float32 [1024, 2], P('groups'), parts along dimension 0, may hold values from -1 to 1
- angle_weight: float32 [2, 4096], P(None, 'fsdp'), may hold values from -3 to 3
- target: bfloat16 [1024, 4096], P('groups', 'fsdp'), parts along dimension 0, may hold values from -6 to 6
- sched: int32 [4], P('section'), may hold values from 0 to 1
Outputs:
- fwd_out: bfloat16 [4, 1024, 4096], P('section', 'groups', 'fsdp'), parts along dimension 1
- grad_in: bfloat16 [4, 1024, 4096], P('section', 'groups', 'fsdp'), parts along dimension 1
- grad_w: bfloat16 [4, 8192, 4096], P('section', 'groups', 'fsdp'), parts along dimension 1
- grad_bias: float32 [4, 8192], P('section', ('groups', 'fsdp')), parts along dimension 1
The draws below stay inside these ranges and needn't reach their ends.
There are 2 independent parts, one for each index of `groups`. The reference program is written for one: setup_inputs(seed, part) draws one part's arguments, and reference() takes and returns one part's arrays. A program takes and returns all parts, laid end to end along the dimension named above; an argument that names none is the same for every part. Nothing has to cross between parts.
All inputs are finite; a program needn't handle non-finite values.
Results may differ from the reference program's by a relative error of at most 0.017.
Values may be sent and summed in bfloat16 or wider, within the bound.
A program may use at most 128 MiB of HBM per device.

```python
import jax
import jax.numpy as jnp
from jax import lax

D = 4096
NSEG = 4784
KACT = 32
MB = 512
NSTASH = 2
N_SECTION = 4
N_FSDP = 4


def draw_sched(key, part):
    offset = jax.random.randint(key, (), 0, NSTASH)
    return jnp.mod(jnp.arange(N_SECTION, dtype=jnp.int32) + offset, NSTASH).astype(jnp.int32)


def draw_sent_grad(key, part):
    noise_key = jax.random.fold_in(key, 11)
    column_key = jax.random.fold_in(key, 12)
    noise = jax.random.normal(noise_key, (N_SECTION, MB, D), jnp.float32)
    column = 0.5 * jax.random.normal(column_key, (N_SECTION, 1, D), jnp.float32)
    return jnp.clip(noise + column, -6.0, 6.0).astype(jnp.bfloat16)


def with_ends(entries, stream_key, least, top_value):
    longest = entries.shape.index(max(entries.shape))
    spots = []
    for shift in (0, 1):
        where = [jax.random.randint(jax.random.fold_in(stream_key, axis), (), 0, length) for axis, length in enumerate(entries.shape)]
        where[longest] = (where[longest] + shift) % entries.shape[longest]
        spots.append(tuple(where))
    return entries.at[spots[0]].set(least).at[spots[1]].set(top_value)


def strengthened(array, own_key, source, target, parts, factor):
    owner, partner = [(jnp.arange(array.shape[dim]) // (array.shape[dim] // parts)).reshape([-1 if axis == dim else 1 for axis in range(array.ndim)]) for dim in (source, target)]
    chosen = jax.random.permutation(own_key, parts)[partner]
    strong = (owner == chosen) | (owner == (partner + parts // 2) % parts)
    return jnp.where(strong, factor * array, array)


def block_levels(key, extent, shards, smallest, high):
    def one(position, blocks):
        steps = jax.random.uniform(jax.random.fold_in(jax.random.fold_in(key, 6), position), (blocks,), jnp.float32, smallest / len(shards), high / len(shards))
        return jnp.repeat(jnp.exp(steps), extent[position] // blocks).reshape((-1,) + (1,) * (len(extent) - position - 1))

    factor_of = one(*shards[0])
    for cut in shards[1:]:
        factor_of = factor_of * one(*cut)
    return factor_of


def bell_draw(key, dims, scale, reach, pieces=(), kind=jnp.bfloat16):
    values = scale * jax.random.normal(key, dims, jnp.float32)
    if pieces:
        values = values * block_levels(key, dims, pieces, -0.22, 0.18)
    return jnp.clip(values, -reach, reach).astype(kind)


def noise_with(rng, extent, scale, bound, shards, heavy, kind=jnp.bfloat16):
    array = scale * jax.random.normal(rng, extent, jnp.float32)
    if shards:
        array = array * block_levels(rng, extent, shards, -0.22, 0.18)
    return jnp.clip(strengthened(array, jax.random.fold_in(rng, 3), *heavy), -bound, bound).astype(kind)


def setup_inputs(seed: int = 0, part: int = 0) -> dict:
    splits = jax.random.split(jax.random.key(seed), 14)
    part_splits = jax.random.split(jax.random.fold_in(splits[13], part), 14)
    return {
        "sent_act": bell_draw(part_splits[0], (N_SECTION, MB, D), 1.0, 6.0, ((0, 4), (2, 4))),
        "sent_grad": draw_sent_grad(jax.random.fold_in(jax.random.fold_in(splits[13], part), 71), part),
        "stash_in": bell_draw(part_splits[2], (N_SECTION, NSTASH, MB, D), 1.0, 6.0, ((0, 4), (3, 4))),
        "stash_pre": bell_draw(part_splits[3], (N_SECTION, NSTASH, MB, D), 1.0, 6.0, ((0, 4), (3, 4))),
        "layer_weight": noise_with(splits[4], (N_SECTION, D, D), D ** -0.5, 0.125, ((0, 4), (2, 4)), (2, 1, 4, 2.0)),
        "layer_bias": bell_draw(splits[5], (N_SECTION, D), 0.5, 3.0, ((0, 4), (1, 4)), jnp.float32),
        "seg_table": bell_draw(splits[6], (NSEG, D), 1.0, 6.0, ((0, 4), (1, 4))),
        "seg_index": with_ends(jax.random.randint(part_splits[7], (MB, KACT), 0, NSEG), jax.random.fold_in(part_splits[7], 1), 0, NSEG - 1).astype(jnp.int32),
        "seg_amp": bell_draw(part_splits[8], (MB, KACT), 0.2, 1.2, (), jnp.float32),
        "field_angle": jnp.clip(jax.random.uniform(part_splits[9], (MB, 2), jnp.float32, -1.0, 1.0), -1.0, 1.0),
        "angle_weight": bell_draw(splits[10], (2, D), 0.5, 3.0, ((1, 4),), jnp.float32),
        "target": bell_draw(part_splits[11], (MB, D), 1.0, 6.0, ((1, 4),)),
        "sched": draw_sched(jax.random.fold_in(splits[13], 71), part),
    }


def gelu_back(stashed_pre, target_rows, cotangent_in, is_last):
    stashed_f32 = stashed_pre.astype(jnp.float32)
    stashed_act, pullback = jax.vjp(jax.nn.gelu, stashed_f32)
    if is_last:
        cotangent = stashed_act - target_rows.astype(jnp.float32)
    else:
        cotangent = cotangent_in.astype(jnp.float32)
    return pullback(cotangent)[0].astype(jnp.bfloat16)

def reference(sent_act, sent_grad, stash_in, stash_pre, layer_weight, layer_bias, seg_table, seg_index, seg_amp, field_angle, angle_weight, target, sched):
    embedded = jnp.zeros((MB, D), jnp.float32)
    for column in range(KACT):
        picked = jnp.take(seg_table, seg_index[:, column], axis=0).astype(jnp.float32)
        embedded = embedded + seg_amp[:, column:column + 1] * picked
    angular = jnp.dot(field_angle, angle_weight, precision=lax.Precision.HIGHEST)
    first_input = (embedded + angular).astype(jnp.bfloat16)
    width = D // N_FSDP
    outputs, input_grads, weight_grads, bias_grads = ([], [], [], [])
    for section_num in range(N_SECTION):
        layer_input = first_input if section_num == 0 else sent_act[section_num - 1]
        preact = jnp.dot(layer_input, layer_weight[section_num], preferred_element_type=jnp.float32) + layer_bias[section_num]
        outputs.append(jax.nn.gelu(preact).astype(jnp.bfloat16))
        stash_slot = sched[section_num]
        stashed_in = stash_in[section_num][stash_slot]
        stashed_pre = stash_pre[section_num][stash_slot]
        following = sent_grad[min(section_num + 1, N_SECTION - 1)]
        pre_grad = gelu_back(stashed_pre, target, following, section_num == N_SECTION - 1)
        weight_grads.append(jnp.dot(stashed_in.T, pre_grad, preferred_element_type=jnp.float32).astype(jnp.bfloat16))
        bias_grads.append(lax.optimization_barrier(jnp.sum(pre_grad.astype(jnp.float32), axis=0)))
        summed = jnp.zeros((MB, D), jnp.float32)
        for shard_num in range(N_FSDP):
            lower = shard_num * width
            input_part = jnp.dot(pre_grad[:, lower:lower + width], layer_weight[section_num][:, lower:lower + width].T, preferred_element_type=jnp.float32).astype(jnp.bfloat16)
            summed = summed + input_part.astype(jnp.float32)
        input_grads.append(summed.astype(jnp.bfloat16))
    return (jnp.stack(outputs), jnp.stack(input_grads), jnp.stack(weight_grads), jnp.stack(bias_grads))
```

```python
import jax
import jax.numpy as jnp
from jax import lax
from jax.experimental import pallas as pl
from jax.experimental.pallas import tpu as pltpu
from jax.sharding import PartitionSpec as P


def from_behind(shard, axis, by):
    length = lax.axis_size(axis)
    pairs = [(i, i + by) for i in range(length) if 0 <= i + by < length]
    return lax.ppermute(shard, axis, pairs)


def embed_rows(row_block, local_ref, amp_ref, matrix_ref):
    begin = pl.multiple_of(row_block * 16, 16)
    wide = matrix_ref.shape[1]
    ids = local_ref[pl.ds(begin, 16), :]
    amps = amp_ref[pl.ds(begin, 16), :]
    position = lax.broadcasted_iota(jnp.int32, (16, wide), 1)
    total = jnp.zeros((16, wide), jnp.float32)
    for k in range(local_ref.shape[1]):
        total = total + jnp.where(ids[:, k : k + 1] == position, amps[:, k : k + 1], 0.0)
    matrix_ref[pl.ds(begin, 16), :] = total.astype(jnp.bfloat16)


def embed_kernel(local_ref, amp_ref, table_ref, out_ref, matrix_ref):
    rows = table_ref.shape[0]

    def step(row_block, carry):
        embed_rows(row_block, local_ref, amp_ref, matrix_ref)
        return carry

    lax.fori_loop(0, local_ref.shape[0] // 16, step, 0)
    out_ref[...] = jnp.dot(
        matrix_ref[:, :rows], table_ref[...], preferred_element_type=jnp.float32
    ).astype(jnp.bfloat16)


def lookup_sum(table, seg_index, seg_amp, first_row):
    samples = seg_index.shape[0]
    rows, width = table.shape
    wide = (rows + 127) // 128 * 128
    return pl.pallas_call(
        embed_kernel,
        out_shape=jax.ShapeDtypeStruct((samples, width), jnp.bfloat16),
        in_specs=[pl.BlockSpec(memory_space=pltpu.VMEM)] * 3,
        out_specs=pl.BlockSpec(memory_space=pltpu.VMEM),
        scratch_shapes=[pltpu.VMEM((samples, wide), jnp.bfloat16)],
        compiler_params=pltpu.CompilerParams(vmem_limit_bytes=32 * 1024 * 1024),
        cost_estimate=pl.CostEstimate(
            flops=2 * samples * rows * width, bytes_accessed=4 * rows * width, transcendentals=0
        ),
    )(seg_index - first_row, seg_amp, table)


def local(
    sent_act,
    sent_grad,
    stash_in,
    stash_pre,
    layer_weight,
    layer_bias,
    seg_table,
    seg_index,
    seg_amp,
    field_angle,
    angle_weight,
    target,
    sched,
):
    section_index = lax.axis_index("section")
    section_count = lax.axis_size("section")
    partial_value = lookup_sum(seg_table, seg_index, seg_amp, section_index * seg_table.shape[0])
    embedded = lax.psum(partial_value.astype(jnp.bfloat16), "section").astype(jnp.float32)
    angular = jnp.dot(field_angle, angle_weight, precision=lax.Precision.HIGHEST)
    first_input = (embedded + angular).astype(jnp.bfloat16)
    arrived = from_behind(sent_act[0], "section", 1)
    layer_input = jnp.where(section_index == 0, first_input, arrived)
    from_next = from_behind(sent_grad[0], "section", -1)
    stash_slot = sched[0]
    stashed_in = lax.dynamic_index_in_dim(stash_in[0], stash_slot, 0, keepdims=False)
    stashed_pre = lax.dynamic_index_in_dim(stash_pre[0], stash_slot, 0, keepdims=False)
    stashed_act, pullback = jax.vjp(jax.nn.gelu, stashed_pre.astype(jnp.float32))
    cotangent = jnp.where(
        section_index == section_count - 1,
        stashed_act - target.astype(jnp.float32),
        from_next.astype(jnp.float32),
    )
    pre_grad = pullback(cotangent)[0].astype(jnp.bfloat16)
    grad_bias = jnp.sum(pre_grad.astype(jnp.float32), axis=0)
    weight = layer_weight[0]
    pre_total = jnp.dot(
        lax.all_gather(layer_input, "fsdp", axis=1, tiled=True),
        weight,
        preferred_element_type=jnp.float32,
    )
    grad_total = lax.dot_general(
        lax.all_gather(stashed_in, "fsdp", axis=1, tiled=True),
        pre_grad,
        (((0,), (0,)), ((), ())),
        preferred_element_type=jnp.float32,
    )
    fwd_out = jax.nn.gelu(pre_total + layer_bias[0]).astype(jnp.bfloat16)
    partial_terms = lax.dot_general(
        pre_grad, weight, (((1,), (1,)), ((), ())), preferred_element_type=jnp.float32
    )
    grad_in = lax.psum_scatter(
        partial_terms.astype(jnp.bfloat16), "fsdp", scatter_dimension=1, tiled=True
    )
    return (fwd_out[None], grad_in[None], grad_total.astype(jnp.bfloat16)[None], grad_bias[None])


def solution(mesh):
    return jax.shard_map(
        local,
        mesh=mesh,
        in_specs=(
            P("section", "groups", "fsdp"),
            P("section", "groups", "fsdp"),
            P("section", None, "groups", "fsdp"),
            P("section", None, "groups", "fsdp"),
            P("section", None, "fsdp"),
            P("section", "fsdp"),
            P("section", "fsdp"),
            P("groups", None),
            P("groups", None),
            P("groups", None),
            P(None, "fsdp"),
            P("groups", "fsdp"),
            P("section"),
        ),
        out_specs=(
            P("section", "groups", "fsdp"),
            P("section", "groups", "fsdp"),
            P("section", "groups", "fsdp"),
            P("section", ("groups", "fsdp")),
        ),
        check_vma=False,
    )
```

```python
import functools

import jax
import jax.numpy as jnp
from jax import lax
from jax.experimental import pallas as pl
from jax.experimental.pallas import tpu as pltpu
from jax.sharding import PartitionSpec as P

CHUNKS = 4
MESH = pl.DeviceIdType.MESH
ROOT = 0.7978845608028654
CUBIC = 0.044715


def gelu_parts(x):
    squared = x * x
    t = jnp.tanh(ROOT * (x + CUBIC * x * squared))
    half = 0.5 * (1.0 + t)
    slope = half + 0.5 * x * (1.0 - t * t) * (ROOT * (1.0 + 3.0 * CUBIC * squared))
    return x * half, slope


def gelu(x):
    return x * (0.5 * (1.0 + jnp.tanh(ROOT * (x + CUBIC * x * x * x))))


def kernel(
    sections, shards,
    act_hbm, grad_hbm, stash_ref, pre_ref, weight_hbm, bias_ref, table_ref, index_ref, amp_ref,
    field_ref, angle_ref, target_ref, sched_ref,
    fwd_ref, grad_in_ref, grad_w_hbm, grad_bias_ref,
    weight, feat, stash, from_next, matrix, emb, emb_recv, emb_send, pre_grad,
    part_send, part_recv, own, x_recv, grad_w,
    load_sem, z_send, z_recv, near_send, near_recv, far_send, far_recv, pass_send, pass_recv,
    part_send_sem, part_recv_sem, sum_send_sem, sum_recv_sem, store_sem,
):
    me = lax.axis_index("fsdp")
    sec = lax.axis_index("section")
    chips = shards // 2
    chip, core = me // 2, lax.rem(me, 2)
    partner = chip * 2 + 1 - core
    rows, width = pre_grad.shape
    part = rows // CHUNKS
    tile = min(256, width)

    def at_chip(j, c):
        return lax.rem(chip + j, chips) * 2 + c

    def span(c):
        return pl.ds(c * part, part)

    def remote(src, dst, send, recv, **where):
        return pltpu.make_async_remote_copy(
            src_ref=src, dst_ref=dst, send_sem=send, recv_sem=recv,
            device_id=where, device_id_type=MESH,
        )

    not_last = sec < sections - 1
    not_first = sec > 0

    load = pltpu.make_async_copy(weight_hbm.at[0], weight, load_sem)
    load.start()

    barrier = pltpu.get_barrier_semaphore()
    pl.semaphore_signal(barrier, inc=1, device_id={"fsdp": partner}, device_id_type=MESH)
    for j in range(1, chips):
        pl.semaphore_signal(barrier, inc=1, device_id={"fsdp": at_chip(j, core)}, device_id_type=MESH)

    @pl.when(not_last)
    def _():
        pl.semaphore_signal(barrier, inc=1, device_id={"section": sec + 1}, device_id_type=MESH)

    @pl.when(not_first)
    def _():
        pl.semaphore_signal(barrier, inc=1, device_id={"section": sec - 1}, device_id_type=MESH)

    pl.semaphore_wait(barrier, chips + jnp.where(not_last, 1, 0) + jnp.where(not_first, 1, 0))

    def act_copy(c):
        return remote(act_hbm.at[0, span(c)], feat.at[me, span(c)], z_send.at[0, c], z_recv.at[0, c], section=sec + 1)

    def grad_copy(c):
        return remote(grad_hbm.at[0, span(c)], from_next.at[span(c)], z_send.at[1, c], z_recv.at[1, c], section=sec - 1)

    def emb_copy(c):
        return remote(emb_send.at[span(c)], emb_recv.at[span(c)], z_send.at[2, c], z_recv.at[2, c], section=sec - 1)

    @pl.when(not_first)
    def _():
        for c in range(CHUNKS):
            grad_copy(c).start()

    @pl.when(not_last)
    def _():
        for c in range(CHUNKS):
            act_copy(c).start()

    def near_copy(g, buf, c, block):
        return remote(buf.at[block, span(c)], buf.at[block, span(c)], near_send.at[g, c], near_recv.at[g, c], fsdp=partner)

    def far_copy(g, buf, c, j, block):
        return remote(buf.at[block, span(c)], buf.at[block, span(c)], far_send.at[g, c, j - 1], far_recv.at[g, c, j - 1], fsdp=at_chip(j, core))

    def pass_copy(g, buf, c, j, block):
        return remote(buf.at[block, span(c)], buf.at[block, span(c)], pass_send.at[g, c, j - 1], pass_recv.at[g, c, j - 1], fsdp=partner)

    def gather_start(g, buf, c):
        for j in range(1, chips):
            far_copy(g, buf, c, j, me).start()
        near_copy(g, buf, c, me).start()

    def gather_pass(g, buf, c):
        for j in range(1, chips):
            block = at_chip(chips - j, core)
            far_copy(g, buf, c, j, block).wait_recv()
            pass_copy(g, buf, c, j, block).start()

    def gather_end(g, buf, c):
        near_copy(g, buf, c, partner).wait_recv()
        for j in range(1, chips):
            pass_copy(g, buf, c, j, at_chip(chips - j, 1 - core)).wait_recv()

    def gather_drain(g, buf, c):
        near_copy(g, buf, c, me).wait_send()
        for j in range(1, chips):
            far_copy(g, buf, c, j, me).wait_send()
            pass_copy(g, buf, c, j, at_chip(chips - j, core)).wait_send()

    slot = sched_ref[0]
    for c in range(CHUNKS):
        stash[me, span(c), :] = jnp.where(slot == 0, stash_ref[0, 0, span(c), :], stash_ref[0, 1, span(c), :])
        gather_start(0, stash, c)

    table_rows = table_ref.shape[0]
    wide = matrix.shape[1]
    base = sec * table_rows

    def amplitudes(i, carry):
        begin = pl.multiple_of(i * 16, 16)
        ids = index_ref[pl.ds(begin, 16), :]
        amps = amp_ref[pl.ds(begin, 16), :]
        position = lax.broadcasted_iota(jnp.int32, (16, wide), 1) + base
        total = jnp.zeros((16, wide), jnp.float32)
        for k in range(index_ref.shape[1]):
            total = total + jnp.where(ids[:, k : k + 1] == position, amps[:, k : k + 1], 0.0)
        matrix[pl.ds(begin, 16), :] = total.astype(jnp.bfloat16)
        return carry

    for c in range(CHUNKS):
        lax.fori_loop(c * part // 16, (c + 1) * part // 16, amplitudes, 0)
        emb[span(c), :] = jnp.dot(
            matrix[span(c), :table_rows], table_ref[...], preferred_element_type=jnp.float32
        )

        @pl.when(jnp.logical_not(not_last))
        def _():
            emb_send[span(c), :] = emb[span(c), :].astype(jnp.bfloat16)
            emb_copy(c).start()

    grad_bias_ref[...] = jnp.zeros_like(grad_bias_ref)
    for c in range(CHUNKS):
        @pl.when(not_last)
        def _():
            grad_copy(c).wait_recv()

        def backward(i, carry):
            at = pl.ds(pl.multiple_of(c * part + i * 16, 16), 16)
            saved = jnp.where(slot == 0, pre_ref[0, 0, at, :], pre_ref[0, 1, at, :]).astype(jnp.float32)
            value, slope = gelu_parts(saved)
            cotangent = jnp.where(
                not_last, from_next[at, :].astype(jnp.float32), value - target_ref[at, :].astype(jnp.float32)
            )
            result = (cotangent * slope).astype(jnp.bfloat16)
            pre_grad[at, :] = result
            grad_bias_ref[...] += jnp.sum(result.astype(jnp.float32), axis=0, keepdims=True)
            return carry

        lax.fori_loop(0, part // 16, backward, 0)

        @pl.when(not_first)
        def _():
            act_copy(c).wait_recv()
            gather_start(1, feat, c)

    load.wait()

    def input_part(j, c, into):
        block = at_chip(j, c)

        def step(t, carry):
            begin = pl.multiple_of(block * width + t * tile, tile)
            column = pl.ds(pl.multiple_of(t * tile, tile), tile)
            into[j, :, column] = lax.dot_general(
                pre_grad[...], weight[pl.ds(begin, tile), :], (((1,), (1,)), ((), ())),
                preferred_element_type=jnp.float32,
            ).astype(jnp.bfloat16)
            return carry

        lax.fori_loop(0, width // tile, step, 0)

    def part_copy(j):
        return remote(part_send.at[j], part_recv.at[j], part_send_sem.at[j], part_recv_sem.at[j], fsdp=partner)

    def sum_copy(j):
        return remote(own.at[j], x_recv.at[j - 1], sum_send_sem.at[j - 1], sum_recv_sem.at[j - 1], fsdp=at_chip(j, core))

    def chain(c):
        @pl.when(not_last)
        def _():
            emb_copy(c).wait_recv()

            def add(i, carry):
                at = pl.ds(pl.multiple_of(c * part + i * 16, 16), 16)
                total = emb[at, :] + emb_recv[at, :].astype(jnp.float32)

                @pl.when(not_first)
                def _():
                    emb_send[at, :] = total.astype(jnp.bfloat16)

                @pl.when(sec == 0)
                def _():
                    angular = (
                        field_ref[at, 0:1] * angle_ref[0:1, :] + field_ref[at, 1:2] * angle_ref[1:2, :]
                    )
                    feat[me, at, :] = (total + angular).astype(jnp.bfloat16)

                return carry

            lax.fori_loop(0, part // 16, add, 0)

            @pl.when(not_first)
            def _():
                emb_copy(c).start()

            @pl.when(sec == 0)
            def _():
                gather_start(1, feat, c)

    for j in range(1, chips):
        input_part(j, 1 - core, part_send)
        part_copy(j).start()
    for j in range(1, chips):
        input_part(j, core, own)
        part_copy(j).wait_recv()
        for c in range(CHUNKS):
            own[j, span(c), :] = (
                own[j, span(c), :].astype(jnp.float32) + part_recv[j, span(c), :].astype(jnp.float32)
            ).astype(jnp.bfloat16)
        sum_copy(j).start()
    chain(0)
    input_part(0, 1 - core, part_send)
    part_copy(0).start()
    chain(1)
    input_part(0, core, own)
    chain(2)

    def store_copy(block):
        at = pl.ds(pl.multiple_of(block * width, width), width)
        return pltpu.make_async_copy(grad_w.at[at, :], grad_w_hbm.at[0, at, :], store_sem.at[block])

    def weight_grad(block):
        def step(t, carry):
            begin = pl.multiple_of(block * width + t * tile, tile)
            column = pl.ds(pl.multiple_of(t * tile, tile), tile)
            grad_w[pl.ds(begin, tile), :] = lax.dot_general(
                stash[block, :, column], pre_grad[...], (((0,), (0,)), ((), ())),
                preferred_element_type=jnp.float32,
            ).astype(jnp.bfloat16)
            return carry

        lax.fori_loop(0, width // tile, step, 0)
        store_copy(block).start()

    for c in range(CHUNKS):
        gather_pass(0, stash, c)
    weight_grad(me)
    chain(3)
    for c in range(CHUNKS):
        gather_end(0, stash, c)
    weight_grad(partner)
    for j in range(1, chips):
        weight_grad(at_chip(j, core))
        weight_grad(at_chip(j, 1 - core))

    def forward(c):
        total = jnp.zeros((part, width), jnp.float32)
        for b in range(shards):
            total = total + jnp.dot(
                feat[b, span(c), :], weight[b * width : (b + 1) * width, :],
                preferred_element_type=jnp.float32,
            )
        fwd_ref[0, span(c), :] = gelu(total + bias_ref[...]).astype(jnp.bfloat16)

    for c in range(CHUNKS):
        gather_pass(1, feat, c)
        if c > 0:
            gather_end(1, feat, c - 1)
            forward(c - 1)
    gather_end(1, feat, CHUNKS - 1)
    forward(CHUNKS - 1)

    part_copy(0).wait_recv()
    for j in range(1, chips):
        sum_copy(j).wait_recv()
    for c in range(CHUNKS):
        total = own[0, span(c), :].astype(jnp.float32) + part_recv[0, span(c), :].astype(jnp.float32)
        for j in range(1, chips):
            total = total + x_recv[j - 1, span(c), :].astype(jnp.float32)
        grad_in_ref[0, span(c), :] = total.astype(jnp.bfloat16)

    for c in range(CHUNKS):
        gather_drain(0, stash, c)
        gather_drain(1, feat, c)
    for j in range(chips):
        part_copy(j).wait_send()
    for j in range(1, chips):
        sum_copy(j).wait_send()
    for b in range(shards):
        store_copy(b).wait()

    @pl.when(not_last)
    def _():
        for c in range(CHUNKS):
            act_copy(c).wait_send()

    @pl.when(not_first)
    def _():
        for c in range(CHUNKS):
            grad_copy(c).wait_send()
            emb_copy(c).wait_send()


def local(sections, shards, *args):
    rows, width = args[0].shape[1:]
    table_rows = args[6].shape[0]
    wide = (table_rows + 127) // 128 * 128
    chips = shards // 2
    vmem = pl.BlockSpec(memory_space=pltpu.VMEM)
    hbm = pl.BlockSpec(memory_space=pl.ANY)
    smem = pl.BlockSpec(memory_space=pltpu.SMEM)
    dma = pltpu.SemaphoreType.DMA
    half, full = jnp.bfloat16, jnp.float32
    return pl.pallas_call(
        functools.partial(kernel, sections, shards),
        out_shape=(
            jax.ShapeDtypeStruct((1, rows, width), half),
            jax.ShapeDtypeStruct((1, rows, width), half),
            jax.ShapeDtypeStruct((1, shards * width, width), half),
            jax.ShapeDtypeStruct((1, width), full),
        ),
        in_specs=[hbm, hbm, vmem, vmem, hbm] + [vmem] * 7 + [smem],
        out_specs=(vmem, vmem, hbm, vmem),
        scratch_shapes=[
            pltpu.VMEM((shards * width, width), half),
            pltpu.VMEM((shards, rows, width), half),
            pltpu.VMEM((shards, rows, width), half),
            pltpu.VMEM((rows, width), half),
            pltpu.VMEM((rows, wide), half),
            pltpu.VMEM((rows, width), full),
            pltpu.VMEM((rows, width), half),
            pltpu.VMEM((rows, width), half),
            pltpu.VMEM((rows, width), half),
            pltpu.VMEM((chips, rows, width), half),
            pltpu.VMEM((chips, rows, width), half),
            pltpu.VMEM((chips, rows, width), half),
            pltpu.VMEM((chips - 1, rows, width), half),
            pltpu.VMEM((shards * width, width), half),
            dma,
            dma((3, CHUNKS)),
            dma((3, CHUNKS)),
            dma((2, CHUNKS)),
            dma((2, CHUNKS)),
            dma((2, CHUNKS, chips - 1)),
            dma((2, CHUNKS, chips - 1)),
            dma((2, CHUNKS, chips - 1)),
            dma((2, CHUNKS, chips - 1)),
            dma((chips,)),
            dma((chips,)),
            dma((chips - 1,)),
            dma((chips - 1,)),
            dma((shards,)),
        ],
        compiler_params=pltpu.CompilerParams(
            collective_id=0, has_side_effects=True, vmem_limit_bytes=60 * 1024 * 1024
        ),
        cost_estimate=pl.CostEstimate(
            flops=6 * rows * shards * width * width, bytes_accessed=40 * rows * width, transcendentals=0
        ),
    )(*args)


def solution(mesh):
    return jax.shard_map(
        functools.partial(local, mesh.shape["section"], mesh.shape["fsdp"]),
        mesh=mesh,
        in_specs=(
            P("section", "groups", "fsdp"),
            P("section", "groups", "fsdp"),
            P("section", None, "groups", "fsdp"),
            P("section", None, "groups", "fsdp"),
            P("section", None, "fsdp"),
            P("section", "fsdp"),
            P("section", "fsdp"),
            P("groups", None),
            P("groups", None),
            P("groups", None),
            P(None, "fsdp"),
            P("groups", "fsdp"),
            P("section"),
        ),
        out_specs=(
            P("section", "groups", "fsdp"),
            P("section", "groups", "fsdp"),
            P("section", "groups", "fsdp"),
            P("section", ("groups", "fsdp")),
        ),
        check_vma=False,
    )
```

```python
import functools

import jax
import jax.numpy as jnp
from jax import lax
from jax.experimental import pallas as pl
from jax.experimental.pallas import tpu as pltpu
from jax.sharding import PartitionSpec as P

CHUNKS = 4
MESH = pl.DeviceIdType.MESH
ROOT = 0.7978845608028654
CUBIC = 0.044715


def gelu_parts(x):
    squared = x * x
    t = jnp.tanh(ROOT * (x + CUBIC * x * squared))
    half = 0.5 * (1.0 + t)
    slope = half + 0.5 * x * (1.0 - t * t) * (ROOT * (1.0 + 3.0 * CUBIC * squared))
    return x * half, slope


def gelu(x):
    return x * (0.5 * (1.0 + jnp.tanh(ROOT * (x + CUBIC * x * x * x))))


def kernel(
    sections, shards,
    act_hbm, grad_hbm, stash_ref, pre_ref, weight_hbm, bias_ref, table_ref, index_in, amp_in,
    field_in, angle_ref, target_ref, sched_ref,
    fwd_ref, grad_in_ref, grad_w_hbm, grad_bias_ref,
    weight, feat, stash, from_next, matrix, emb, emb_recv, emb_send, pre_grad,
    part_send, part_recv, own, x_recv, grad_w,
    index_ref, amp_ref, field_ref,
    load_sem, z_send, z_recv, near_send, near_recv, far_send, far_recv, pass_send, pass_recv,
    part_send_sem, part_recv_sem, sum_send_sem, sum_recv_sem, store_sem,
):
    me = lax.axis_index("fsdp")
    sec = lax.axis_index("section")
    chips = shards // 2
    chip, core = me // 2, lax.rem(me, 2)
    partner = chip * 2 + 1 - core
    rows, width = pre_grad.shape
    part = rows // CHUNKS
    tile = min(256, width)

    def at_chip(j, c):
        return lax.rem(chip + j, chips) * 2 + c

    def span(c):
        return pl.ds(c * part, part)

    def remote(src, dst, send, recv, **where):
        return pltpu.make_async_remote_copy(
            src_ref=src, dst_ref=dst, send_sem=send, recv_sem=recv,
            device_id=where, device_id_type=MESH,
        )

    not_last = sec < sections - 1
    not_first = sec > 0

    load = pltpu.make_async_copy(weight_hbm.at[0], weight, load_sem)
    load.start()

    barrier = pltpu.get_barrier_semaphore()
    pl.semaphore_signal(barrier, inc=1, device_id={"fsdp": partner}, device_id_type=MESH)
    for j in range(1, chips):
        pl.semaphore_signal(barrier, inc=1, device_id={"fsdp": at_chip(j, core)}, device_id_type=MESH)

    @pl.when(not_last)
    def _():
        pl.semaphore_signal(barrier, inc=1, device_id={"section": sec + 1}, device_id_type=MESH)

    @pl.when(not_first)
    def _():
        pl.semaphore_signal(barrier, inc=1, device_id={"section": sec - 1}, device_id_type=MESH)

    pl.semaphore_wait(barrier, chips + jnp.where(not_last, 1, 0) + jnp.where(not_first, 1, 0))

    def act_copy(c):
        return remote(act_hbm.at[0, span(c)], feat.at[me, span(c)], z_send.at[0, c], z_recv.at[0, c], section=sec + 1)

    def grad_copy(c):
        return remote(grad_hbm.at[0, span(c)], from_next.at[span(c)], z_send.at[1, c], z_recv.at[1, c], section=sec - 1)

    def emb_copy(c):
        return remote(emb_send.at[span(c)], emb_recv.at[span(c)], z_send.at[2, c], z_recv.at[2, c], section=sec - 1)

    @pl.when(not_first)
    def _():
        for c in range(CHUNKS):
            grad_copy(c).start()

    @pl.when(not_last)
    def _():
        for c in range(CHUNKS):
            act_copy(c).start()

    def near_copy(g, buf, c, block):
        return remote(buf.at[block, span(c)], buf.at[block, span(c)], near_send.at[g, c], near_recv.at[g, c], fsdp=partner)

    def far_copy(g, buf, c, j, block):
        return remote(buf.at[block, span(c)], buf.at[block, span(c)], far_send.at[g, c, j - 1], far_recv.at[g, c, j - 1], fsdp=at_chip(j, core))

    def pass_copy(g, buf, c, j, block):
        return remote(buf.at[block, span(c)], buf.at[block, span(c)], pass_send.at[g, c, j - 1], pass_recv.at[g, c, j - 1], fsdp=partner)

    def gather_start(g, buf, c):
        for j in range(1, chips):
            far_copy(g, buf, c, j, me).start()
        near_copy(g, buf, c, me).start()

    def gather_pass(g, buf, c):
        for j in range(1, chips):
            block = at_chip(chips - j, core)
            far_copy(g, buf, c, j, block).wait_recv()
            pass_copy(g, buf, c, j, block).start()

    def gather_end(g, buf, c):
        near_copy(g, buf, c, partner).wait_recv()
        for j in range(1, chips):
            pass_copy(g, buf, c, j, at_chip(chips - j, 1 - core)).wait_recv()

    def gather_drain(g, buf, c):
        near_copy(g, buf, c, me).wait_send()
        for j in range(1, chips):
            far_copy(g, buf, c, j, me).wait_send()
            pass_copy(g, buf, c, j, at_chip(chips - j, core)).wait_send()

    slot = sched_ref[0]
    for c in range(CHUNKS):
        stash[me, span(c), :] = jnp.where(slot == 0, stash_ref[0, 0, span(c), :], stash_ref[0, 1, span(c), :])
        gather_start(0, stash, c)

    for c in range(rows // 128):
        at = pl.ds(c * 128, 128)
        index_ref[at, :] = index_in[:, at].T
        amp_ref[at, :] = amp_in[:, at].T
        field_ref[at, :] = field_in[:, at].T

    table_rows = table_ref.shape[0]
    wide = matrix.shape[1]
    base = sec * table_rows

    def amplitudes(i, carry):
        begin = pl.multiple_of(i * 16, 16)
        ids = index_ref[pl.ds(begin, 16), :]
        amps = amp_ref[pl.ds(begin, 16), :]
        position = lax.broadcasted_iota(jnp.int32, (16, wide), 1) + base
        total = jnp.zeros((16, wide), jnp.float32)
        for k in range(index_ref.shape[1]):
            total = total + jnp.where(ids[:, k : k + 1] == position, amps[:, k : k + 1], 0.0)
        matrix[pl.ds(begin, 16), :] = total.astype(jnp.bfloat16)
        return carry

    for c in range(CHUNKS):
        lax.fori_loop(c * part // 16, (c + 1) * part // 16, amplitudes, 0)
        emb[span(c), :] = jnp.dot(
            matrix[span(c), :table_rows], table_ref[...], preferred_element_type=jnp.float32
        )

        @pl.when(jnp.logical_not(not_last))
        def _():
            emb_send[span(c), :] = emb[span(c), :].astype(jnp.bfloat16)
            emb_copy(c).start()

    grad_bias_ref[...] = jnp.zeros_like(grad_bias_ref)
    for c in range(CHUNKS):
        @pl.when(not_last)
        def _():
            grad_copy(c).wait_recv()

        def backward(i, carry):
            at = pl.ds(pl.multiple_of(c * part + i * 16, 16), 16)
            saved = jnp.where(slot == 0, pre_ref[0, 0, at, :], pre_ref[0, 1, at, :]).astype(jnp.float32)
            value, slope = gelu_parts(saved)
            cotangent = jnp.where(
                not_last, from_next[at, :].astype(jnp.float32), value - target_ref[at, :].astype(jnp.float32)
            )
            result = (cotangent * slope).astype(jnp.bfloat16)
            pre_grad[at, :] = result
            grad_bias_ref[...] += jnp.sum(result.astype(jnp.float32), axis=0, keepdims=True)
            return carry

        lax.fori_loop(0, part // 16, backward, 0)

        @pl.when(not_first)
        def _():
            act_copy(c).wait_recv()
            gather_start(1, feat, c)

    load.wait()

    def input_part(j, c, into):
        block = at_chip(j, c)

        def step(t, carry):
            begin = pl.multiple_of(block * width + t * tile, tile)
            column = pl.ds(pl.multiple_of(t * tile, tile), tile)
            into[j, :, column] = lax.dot_general(
                pre_grad[...], weight[pl.ds(begin, tile), :], (((1,), (1,)), ((), ())),
                preferred_element_type=jnp.float32,
            ).astype(jnp.bfloat16)
            return carry

        lax.fori_loop(0, width // tile, step, 0)

    def part_copy(j):
        return remote(part_send.at[j], part_recv.at[j], part_send_sem.at[j], part_recv_sem.at[j], fsdp=partner)

    def sum_copy(j):
        return remote(own.at[j], x_recv.at[j - 1], sum_send_sem.at[j - 1], sum_recv_sem.at[j - 1], fsdp=at_chip(j, core))

    def chain(c):
        @pl.when(not_last)
        def _():
            emb_copy(c).wait_recv()

            def add(i, carry):
                at = pl.ds(pl.multiple_of(c * part + i * 16, 16), 16)
                total = emb[at, :] + emb_recv[at, :].astype(jnp.float32)

                @pl.when(not_first)
                def _():
                    emb_send[at, :] = total.astype(jnp.bfloat16)

                @pl.when(sec == 0)
                def _():
                    angular = (
                        field_ref[at, 0:1] * angle_ref[0:1, :] + field_ref[at, 1:2] * angle_ref[1:2, :]
                    )
                    feat[me, at, :] = (total + angular).astype(jnp.bfloat16)

                return carry

            lax.fori_loop(0, part // 16, add, 0)

            @pl.when(not_first)
            def _():
                emb_copy(c).start()

            @pl.when(sec == 0)
            def _():
                gather_start(1, feat, c)

    for j in range(1, chips):
        input_part(j, 1 - core, part_send)
        part_copy(j).start()
    for j in range(1, chips):
        input_part(j, core, own)
        part_copy(j).wait_recv()
        for c in range(CHUNKS):
            own[j, span(c), :] = (
                own[j, span(c), :].astype(jnp.float32) + part_recv[j, span(c), :].astype(jnp.float32)
            ).astype(jnp.bfloat16)
        sum_copy(j).start()
    chain(0)
    input_part(0, 1 - core, part_send)
    part_copy(0).start()
    chain(1)
    input_part(0, core, own)
    chain(2)

    def store_copy(block):
        at = pl.ds(pl.multiple_of(block * width, width), width)
        return pltpu.make_async_copy(grad_w.at[at, :], grad_w_hbm.at[0, at, :], store_sem.at[block])

    def weight_grad(block):
        def step(t, carry):
            begin = pl.multiple_of(block * width + t * tile, tile)
            column = pl.ds(pl.multiple_of(t * tile, tile), tile)
            grad_w[pl.ds(begin, tile), :] = lax.dot_general(
                stash[block, :, column], pre_grad[...], (((0,), (0,)), ((), ())),
                preferred_element_type=jnp.float32,
            ).astype(jnp.bfloat16)
            return carry

        lax.fori_loop(0, width // tile, step, 0)
        store_copy(block).start()

    for c in range(CHUNKS):
        gather_pass(0, stash, c)
    weight_grad(me)
    chain(3)
    for c in range(CHUNKS):
        gather_end(0, stash, c)
    weight_grad(partner)
    for j in range(1, chips):
        weight_grad(at_chip(j, core))
        weight_grad(at_chip(j, 1 - core))

    def forward(c):
        total = jnp.zeros((part, width), jnp.float32)
        for b in range(shards):
            total = total + jnp.dot(
                feat[b, span(c), :], weight[b * width : (b + 1) * width, :],
                preferred_element_type=jnp.float32,
            )
        fwd_ref[0, span(c), :] = gelu(total + bias_ref[...]).astype(jnp.bfloat16)

    for c in range(CHUNKS):
        gather_pass(1, feat, c)
        if c > 0:
            gather_end(1, feat, c - 1)
            forward(c - 1)
    gather_end(1, feat, CHUNKS - 1)
    forward(CHUNKS - 1)

    part_copy(0).wait_recv()
    for j in range(1, chips):
        sum_copy(j).wait_recv()
    for c in range(CHUNKS):
        total = own[0, span(c), :].astype(jnp.float32) + part_recv[0, span(c), :].astype(jnp.float32)
        for j in range(1, chips):
            total = total + x_recv[j - 1, span(c), :].astype(jnp.float32)
        grad_in_ref[0, span(c), :] = total.astype(jnp.bfloat16)

    for c in range(CHUNKS):
        gather_drain(0, stash, c)
        gather_drain(1, feat, c)
    for j in range(chips):
        part_copy(j).wait_send()
    for j in range(1, chips):
        sum_copy(j).wait_send()
    for b in range(shards):
        store_copy(b).wait()

    @pl.when(not_last)
    def _():
        for c in range(CHUNKS):
            act_copy(c).wait_send()

    @pl.when(not_first)
    def _():
        for c in range(CHUNKS):
            grad_copy(c).wait_send()
            emb_copy(c).wait_send()


def copy_kernel(pieces, a, b, c, d, a_out, b_out, c_out, d_out, sem):
    copies = []
    for source, target, count in zip((c, a, b), (c_out, a_out, b_out), (pieces[2], pieces[0], pieces[1])):
        size = source.shape[1] // count
        for i in range(count):
            at = pl.ds(i * size, size)
            copies.append(
                pltpu.make_async_copy(source.at[0, at], target.at[0, at], sem.at[len(copies)])
            )
    copies.append(pltpu.make_async_copy(d, d_out, sem.at[len(copies)]))
    for copy in copies:
        copy.start()
    for copy in copies:
        copy.wait()


def local(sections, shards, *args):
    rows, width = args[0].shape[1:]
    table_rows = args[6].shape[0]
    wide = (table_rows + 127) // 128 * 128
    chips = shards // 2
    vmem = pl.BlockSpec(memory_space=pltpu.VMEM)
    hbm = pl.BlockSpec(memory_space=pl.ANY)
    smem = pl.BlockSpec(memory_space=pltpu.SMEM)
    dma = pltpu.SemaphoreType.DMA
    half, full = jnp.bfloat16, jnp.float32
    args = list(args)
    inputs = args[:7] + [args[7].T, args[8].T, jnp.pad(args[9].T, ((0, 6), (0, 0)))] + args[10:]
    results = pl.pallas_call(
        functools.partial(kernel, sections, shards),
        out_shape=(
            jax.ShapeDtypeStruct((1, rows, width), half),
            jax.ShapeDtypeStruct((1, rows, width), half),
            jax.ShapeDtypeStruct((1, shards * width, width), half),
            jax.ShapeDtypeStruct((1, width), full),
        ),
        in_specs=[hbm, hbm, vmem, vmem, hbm] + [vmem] * 7 + [smem],
        out_specs=(vmem, vmem, hbm, vmem),
        scratch_shapes=[
            pltpu.VMEM((shards * width, width), half),
            pltpu.VMEM((shards, rows, width), half),
            pltpu.VMEM((shards, rows, width), half),
            pltpu.VMEM((rows, width), half),
            pltpu.VMEM((rows, wide), half),
            pltpu.VMEM((rows, width), full),
            pltpu.VMEM((rows, width), half),
            pltpu.VMEM((rows, width), half),
            pltpu.VMEM((rows, width), half),
            pltpu.VMEM((chips, rows, width), half),
            pltpu.VMEM((chips, rows, width), half),
            pltpu.VMEM((chips, rows, width), half),
            pltpu.VMEM((chips - 1, rows, width), half),
            pltpu.VMEM((shards * width, width), half),
            pltpu.VMEM((rows, args[7].shape[1]), jnp.int32),
            pltpu.VMEM((rows, args[7].shape[1]), full),
            pltpu.VMEM((rows, 8), full),
            dma,
            dma((3, CHUNKS)),
            dma((3, CHUNKS)),
            dma((2, CHUNKS)),
            dma((2, CHUNKS)),
            dma((2, CHUNKS, chips - 1)),
            dma((2, CHUNKS, chips - 1)),
            dma((2, CHUNKS, chips - 1)),
            dma((2, CHUNKS, chips - 1)),
            dma((chips,)),
            dma((chips,)),
            dma((chips - 1,)),
            dma((chips - 1,)),
            dma((shards,)),
        ],
        compiler_params=pltpu.CompilerParams(
            collective_id=0, has_side_effects=True, vmem_limit_bytes=60 * 1024 * 1024
        ),
        cost_estimate=pl.CostEstimate(
            flops=6 * rows * shards * width * width, bytes_accessed=40 * rows * width, transcendentals=0
        ),
    )(*inputs)
    pieces = (2, 2, 8)
    return pl.pallas_call(
        functools.partial(copy_kernel, pieces),
        out_shape=tuple(jax.ShapeDtypeStruct(r.shape, r.dtype) for r in results),
        in_specs=[hbm] * 4,
        out_specs=(hbm,) * 4,
        scratch_shapes=[dma((sum(pieces) + 1,))],
        cost_estimate=pl.CostEstimate(flops=0, bytes_accessed=40 * rows * width, transcendentals=0),
    )(*results)


def solution(mesh):
    return jax.shard_map(
        functools.partial(local, mesh.shape["section"], mesh.shape["fsdp"]),
        mesh=mesh,
        in_specs=(
            P("section", "groups", "fsdp"),
            P("section", "groups", "fsdp"),
            P("section", None, "groups", "fsdp"),
            P("section", None, "groups", "fsdp"),
            P("section", None, "fsdp"),
            P("section", "fsdp"),
            P("section", "fsdp"),
            P("groups", None),
            P("groups", None),
            P("groups", None),
            P(None, "fsdp"),
            P("groups", "fsdp"),
            P("section"),
        ),
        out_specs=(
            P("section", "groups", "fsdp"),
            P("section", "groups", "fsdp"),
            P("section", "groups", "fsdp"),
            P("section", ("groups", "fsdp")),
        ),
        check_vma=False,
    )
```
